32 devices in a mesh: grp: 2 (over y), pair: 4 (over z), aux: 2 (over x), occ: 2 (over core).
Axes of the slice: x: 2, y: 2, z: 4, core: 2. Of those that a mesh axis runs over, the one named last changes fastest.
Arguments:
- df_ints: bfloat16 [128, 4096, 256], P(('grp', 'pair'), ('aux', 'occ')), parts along dimension 0, may hold values from -2 to 2
- pno_rot: bfloat16 [64, 256, 256], P(('grp', 'pair')), parts along dimension 0, may hold values from -0.375 to 0.375
- margins: bfloat16 [64, 2, 256, 256], P(('grp', 'pair')), parts along dimension 0, may hold values from -0.375 to 0.375
- amplitudes: float32 [64, 256, 256], P(('grp', 'pair'), ('aux', 'occ')), parts along dimension 0, may hold values from -6 to 6
- virt_energy: float32 [64, 256], P(('grp', 'pair')), parts along dimension 0, may hold values from 0.5 to 4
- occ_gap: float32 [64], P(('grp', 'pair')), parts along dimension 0, may hold values from 0.5 to 2
- fock_coupling: float32 [64, 2], P(('grp', 'pair')), parts along dimension 0, may hold values from -3 to 3
- pno_count: int32 [64], P(('grp', 'pair')), parts along dimension 0, may hold values from 64 to 256, as said below
- pair_home: int32 [64, 2], P('grp'), parts along dimension 0, may hold values from 0 to 3, all different within a row; in each aligned block of 8 rows (0 to 7, 8 to 15, ...) at most 6 rows name the same one
- pair_slot: int32 [64, 2], P('grp'), parts along dimension 0, may hold values from 0 to 15
- neigh_home: int32 [64, 2], P('grp'), parts along dimension 0, may hold values from 0 to 3, all different within a row; in each aligned block of 8 rows (0 to 7, 8 to 15, ...) at most 6 rows name the same one
- neigh_slot: int32 [64, 2], P('grp'), parts along dimension 0, may hold values from 0 to 7
Outputs:
- new_amps: float32 [64, 256, 256], P(('grp', 'pair'), ('aux', 'occ')), parts along dimension 0
- pair_energy: float32 [64], P(('grp', 'pair')), parts along dimension 0
The draws below stay inside these ranges and needn't reach their ends.
There are 2 independent parts, one for each index of `grp`. The reference program is written for one: setup_inputs(seed, part) draws one part's arguments, and reference() takes and returns one part's arrays. A program takes and returns all parts, laid end to end along the dimension named above; each array names one. Nothing has to cross between parts.
Inputs may be any that keep to these rules, and one draw needn't show every extreme that they name: `pair_home`: the two entries of a row differ. Among the rows of one owner's 8 pairs (aligned blocks), no value is named more than 6 times, and in some blocks one value is named exactly 6 times; every value is named somewhere. `neigh_home`: the entries of a row differ. Among the rows of one owner's 8 pairs (aligned blocks), no value is named more than 6 times, and in some blocks one value is named exactly 6 times; every value is named somewhere. `pno_count`: A multiple of one quarter of 256.
All inputs are finite; a program needn't handle non-finite values.
Results may differ from the reference program's by a relative error of at most 0.0018.
Values may be sent and summed in bfloat16 or wider, within the bound.
A program may use at most 128 MiB of HBM per device.

```python
import math
import jax
import jax.numpy as jnp
import numpy as np
from jax import lax

A = 256
QDOM = 4096
NB = 2
PAIR_DEV = 8
OCC_DEV = 16
CAP = 6
NPAIR = 32
NOCC = 64
N_PAIR = 4


def draw_pno_count(key, part):
    key = jax.random.fold_in(key, 11)
    return (A // 4 * jax.random.randint(key, (NPAIR,), 1, 5)).astype(jnp.int32)


def with_ends(result, stream_key, low, top_value):
    dims = result.shape
    index_at = [jax.random.randint(jax.random.fold_in(stream_key, axis), (), 0, dims[axis]) for axis in range(len(dims))]
    result = result.at[tuple(index_at)].set(low)
    longest = dims.index(max(dims))
    index_at[longest] = (index_at[longest] + 1) % dims[longest]
    return result.at[tuple(index_at)].set(top_value)


def steps_of(own_key, dims, split, least, top_value):
    def one(dim, parts):
        heights = jax.random.uniform(jax.random.fold_in(jax.random.fold_in(own_key, 6), dim), (parts,), jnp.float32, least / len(split), top_value / len(split))
        return jnp.repeat(jnp.exp(heights), dims[dim] // parts).reshape((-1,) + (1,) * (len(dims) - dim - 1))

    factor_of = one(*split[0])
    for cut in split[1:]:
        factor_of = factor_of * one(*cut)
    return factor_of


def shared_out(own_key, own, number, rows, count, top, most, skew):
    order = jax.random.permutation(own_key, count)
    packed, ordinary = shares(count, rows * top, most, skew, True), shares(count, rows * top, most, skew, False)
    places = jnp.arange(count)

    def named(tallies, offset_by):
        used = int((tallies > 0).sum())
        fixed = max(1, used // 4)
        moved = fixed + (places - fixed + offset_by * (used - fixed)) % max(1, count - fixed)
        return jnp.zeros((count,), jnp.int32).at[order[jnp.where(places < fixed, places, moved)]].set(jnp.asarray(tallies, jnp.int32))

    tallies = jnp.where(number % 4 == 0, named(packed, number // 4), named(ordinary, number - number // 4 - 1))
    mixed = jax.random.permutation(jax.random.fold_in(own, 3), count)
    source_of, taker = mixed[0:count // 2 * 2:2], mixed[1:count // 2 * 2:2]
    room = jnp.minimum(tallies[source_of] - 1, most - tallies[taker]) // 2
    room = jnp.where((source_of == order[0]) | (taker == order[0]) | (tallies[taker] == 0), 0, jnp.maximum(room, 0))
    moved = jax.random.randint(jax.random.fold_in(own, 4), (count // 2,), 0, 1 << 20) % (room + 1)
    tallies = tallies.at[source_of].add(-moved).at[taker].add(moved)
    members = jnp.searchsorted(jnp.cumsum(tallies), jnp.arange(rows * top), side="right").astype(jnp.int32)
    listing = members.reshape(top, rows).T
    listing = listing[jax.random.permutation(jax.random.fold_in(own, 1), rows)]
    offset_by = jax.random.randint(jax.random.fold_in(own, 2), (rows, 1), 0, top)
    return jnp.take_along_axis(listing, (jnp.arange(top)[None, :] + offset_by) % top, axis=1)


def shares(count, total, most, skew, full):
    portions = [(1 << 20) // math.isqrt(rank ** skew) + 1 for rank in range(1, count + 1)]
    largest = most if full else min(most, max(-(-total // count), total * portions[0] // sum(portions)))
    least = 1 if total - largest >= count - 1 else 0
    holding, surplus = [largest] + [least] * (count - 1), total - largest - least * (count - 1)
    while surplus > 0:
        candidates = [i for i in range(1, count) if holding[i] < largest] or [i for i in range(1, count) if holding[i] < most]
        whole, left = sum([portions[i] for i in candidates]), surplus
        for i in candidates:
            extra = min(most - holding[i], max(1, left * portions[i] // whole), surplus)
            holding[i] = holding[i] + extra
            surplus = surplus - extra
    return np.array(holding)


def bell_draw(stream_key, shape, width, bound, shards=(), kind=jnp.bfloat16):
    values = jax.random.normal(stream_key, shape, jnp.float32) * width
    if len(shards) > 0:
        values = steps_of(stream_key, shape, shards, -0.22, 0.18) * values
    return jnp.clip(values, min=-bound, max=bound).astype(kind)


def setup_inputs(seed: int = 0, part: int = 0) -> dict:
    key_of = jax.random.split(jax.random.key(seed), 13)
    own_keys = jax.random.split(jax.random.fold_in(key_of[12], part), 13)
    df_ints = bell_draw(own_keys[0], (NOCC, QDOM, A), 0.125, 2.0, ((0, 4), (1, 4)))
    pno_rot = bell_draw(own_keys[1], (NPAIR, A, A), A ** -0.5, 0.375, ((0, 4),))
    margins = bell_draw(own_keys[2], (NPAIR, NB, A, A), A ** -0.5, 0.375, ((0, 4),))
    amplitudes = bell_draw(own_keys[3], (NPAIR, A, A), 1.0, 6.0, ((0, 4), (1, 4)), jnp.float32)
    virt_energy = jnp.clip(jnp.exp(math.log(4.0) - 2.0794415 * jax.random.uniform(own_keys[4], (NPAIR, A), jnp.float32) ** steps_of(own_keys[4], (NPAIR, A), ((0, 4),), -0.2, 0.2)), 0.5, 4.0)
    occ_gap = jnp.clip(jnp.exp(math.log(2.0) - 1.3862944 * jax.random.uniform(own_keys[5], (NPAIR,), jnp.float32) ** steps_of(own_keys[5], (NPAIR,), ((0, 4),), -0.2, 0.2)), 0.5, 2.0)
    fock_coupling = bell_draw(own_keys[6], (NPAIR, NB), 0.5, 3.0, ((0, 4),), jnp.float32)
    pno_count = draw_pno_count(jax.random.fold_in(jax.random.fold_in(key_of[12], part), 71), part)
    pair_home_keys = jax.random.split(jax.random.fold_in(own_keys[8], 1), NPAIR // PAIR_DEV)
    pair_home_turns = jax.random.permutation(jax.random.fold_in(own_keys[8], 3), NPAIR // PAIR_DEV)
    pair_home = jax.vmap(lambda own, number: shared_out(jax.random.fold_in(own_keys[8], 2), own, number, PAIR_DEV, N_PAIR, 2, CAP, 2))(pair_home_keys, pair_home_turns).reshape((NPAIR, 2))
    pair_slot = with_ends(jax.random.randint(own_keys[9], (NPAIR, 2), 0, OCC_DEV), jax.random.fold_in(own_keys[9], 1), 0, OCC_DEV - 1).astype(jnp.int32)
    neigh_home_keys = jax.random.split(jax.random.fold_in(own_keys[10], 1), NPAIR // PAIR_DEV)
    neigh_home_turns = jax.random.permutation(jax.random.fold_in(own_keys[10], 3), NPAIR // PAIR_DEV)
    neigh_home = jax.vmap(lambda own, number: shared_out(jax.random.fold_in(own_keys[10], 2), own, number, PAIR_DEV, N_PAIR, NB, CAP, 2))(neigh_home_keys, neigh_home_turns).reshape((NPAIR, NB))
    neigh_slot = with_ends(jax.random.randint(own_keys[11], (NPAIR, NB), 0, PAIR_DEV), jax.random.fold_in(own_keys[11], 1), 0, PAIR_DEV - 1).astype(jnp.int32)
    return dict(df_ints=df_ints, pno_rot=pno_rot, margins=margins, amplitudes=amplitudes, virt_energy=virt_energy, occ_gap=occ_gap, fock_coupling=fock_coupling, pno_count=pno_count, pair_home=pair_home, pair_slot=pair_slot, neigh_home=neigh_home, neigh_slot=neigh_slot)


def reference(df_ints, pno_rot, margins, amplitudes, virt_energy, occ_gap, fock_coupling, pno_count, pair_home, pair_slot, neigh_home, neigh_slot):
    orbital = (pair_home * OCC_DEV + pair_slot).astype(jnp.int32)
    partner = (neigh_home * PAIR_DEV + neigh_slot).astype(jnp.int32)
    amp_wire = amplitudes.astype(jnp.bfloat16)
    positions = jnp.arange(A, dtype=jnp.int32)

    def one_pair(pair_index):
        rotation = pno_rot[pair_index]
        left_fit = jnp.dot(df_ints[orbital[pair_index, 0]], rotation, preferred_element_type=jnp.float32).astype(jnp.bfloat16)
        right_fit = jnp.dot(df_ints[orbital[pair_index, 1]], rotation, preferred_element_type=jnp.float32).astype(jnp.bfloat16)
        exchange_int = jnp.dot(left_fit.T, right_fit, preferred_element_type=jnp.float32)
        coupling = jnp.zeros((A, A), jnp.float32)
        for neighbour in range(NB):
            margin = margins[pair_index, neighbour]
            projected = jnp.dot(margin, amp_wire[partner[pair_index, neighbour]], preferred_element_type=jnp.float32).astype(jnp.bfloat16)
            coupling = coupling + fock_coupling[pair_index, neighbour] * jnp.dot(projected, margin.T, preferred_element_type=jnp.float32)
        energies = virt_energy[pair_index]
        denominator = energies[:, None] + energies[None, :] + occ_gap[pair_index]
        current = amplitudes[pair_index]
        residual = exchange_int + denominator * current - coupling
        inside = positions < pno_count[pair_index]
        active = inside[:, None] & inside[None, :]
        updated = jnp.where(active, current - 0.5 * residual / denominator, jnp.zeros_like(current))
        energy = jnp.sum(exchange_int * updated) / A
        return updated, energy

    new_amps, pair_energy = lax.map(one_pair, jnp.arange(NPAIR, dtype=jnp.int32))
    return new_amps, pair_energy
```

```python
import jax
import jax.numpy as jnp
from jax import lax
from jax.sharding import PartitionSpec as P


def body(
    df_ints,
    pno_rot,
    margins,
    amplitudes,
    virt_energy,
    occ_gap,
    fock_coupling,
    pno_count,
    pair_home,
    pair_slot,
    neigh_home,
    neigh_slot,
):
    own_index = lax.axis_index("pair")
    group_index = lax.axis_index(("aux", "occ"))
    pairs_here, pno_width = pno_rot.shape[0], pno_rot.shape[1]
    occ_rows = df_ints.shape[0]
    band_rows = amplitudes.shape[1]
    neigh_count = margins.shape[1]
    orbital = pair_home * occ_rows + pair_slot
    own_homes = lax.dynamic_slice_in_dim(neigh_home, own_index * pairs_here, pairs_here, 0)
    own_slots = lax.dynamic_slice_in_dim(neigh_slot, own_index * pairs_here, pairs_here, 0)
    partner = own_homes * pairs_here + own_slots

    moved = lax.all_to_all(df_ints, "pair", split_axis=1, concat_axis=0, tiled=True)
    rot_all = lax.all_gather(pno_rot, "pair", axis=0, tiled=True)
    blocks = jnp.take(moved, orbital, axis=0)
    fitted = jnp.einsum(
        "peqv,pva->peqa", blocks, rot_all, preferred_element_type=jnp.float32
    ).astype(jnp.bfloat16)
    exchange_part = jnp.einsum(
        "pqa,pqb->pab", fitted[:, 0], fitted[:, 1], preferred_element_type=jnp.float32
    )
    exchange_mid = lax.psum_scatter(
        exchange_part, ("aux", "occ"), scatter_dimension=1, tiled=True
    )
    exchange_rows = lax.psum_scatter(exchange_mid, "pair", scatter_dimension=0, tiled=True)

    amp_all = lax.all_gather(amplitudes.astype(jnp.bfloat16), "pair", axis=0, tiled=True)
    picked = jnp.take(amp_all, partner, axis=0)
    neighbour = lax.all_gather(picked, ("aux", "occ"), axis=2, tiled=True)
    row_start = group_index * band_rows
    margin_rows = lax.dynamic_slice_in_dim(margins, row_start, band_rows, axis=2)
    projected = jnp.einsum(
        "pkrv,pkvb->pkrb", margin_rows, neighbour, preferred_element_type=jnp.float32
    ).astype(jnp.bfloat16)
    coupled = jnp.einsum("pkrb,pkcb->pkrc", projected, margins, preferred_element_type=jnp.float32)
    coupling = jnp.sum(fock_coupling[:, :, None, None] * coupled, axis=1)
    energy_rows = lax.dynamic_slice_in_dim(virt_energy, row_start, band_rows, axis=1)
    denominator = energy_rows[:, :, None] + virt_energy[:, None, :] + occ_gap[:, None, None]
    residual = exchange_rows + denominator * amplitudes - coupling
    row_pos = row_start + jnp.arange(band_rows, dtype=jnp.int32)
    col_pos = jnp.arange(pno_width, dtype=jnp.int32)
    counts = pno_count[:, None, None]
    active = (row_pos[None, :, None] < counts) & (col_pos[None, None, :] < counts)
    updated = jnp.where(
        active, amplitudes - 0.5 * residual / denominator, jnp.zeros_like(amplitudes)
    )
    energy_part = jnp.sum(exchange_rows * updated, axis=(1, 2))
    pair_energy = lax.psum(energy_part, ("aux", "occ")) / pno_width
    return (updated, pair_energy)


def solution(mesh):
    placed = (
        P(("grp", "pair"), ("aux", "occ"), None),
        P(("grp", "pair"), None, None),
        P(("grp", "pair"), None, None, None),
        P(("grp", "pair"), ("aux", "occ"), None),
        P(("grp", "pair"), None),
        P(("grp", "pair")),
        P(("grp", "pair"), None),
        P(("grp", "pair")),
        P("grp", None),
        P("grp", None),
        P("grp", None),
        P("grp", None),
    )
    return jax.shard_map(
        body,
        mesh=mesh,
        in_specs=placed,
        out_specs=(P(("grp", "pair"), ("aux", "occ"), None), P(("grp", "pair"))),
        check_vma=False,
    )
```

```python
import functools

import jax
import jax.numpy as jnp
from jax import lax
from jax.experimental import pallas as pl
from jax.experimental.pallas import tpu as pltpu
from jax.sharding import PartitionSpec as P


MESH = pl.DeviceIdType.MESH


def exchange_kernel(
    sizes, df, rot, idx, out,
    dfb, rotb, ex, crecv, xsend, xrecv, zsend, zrecv,
    local_sem, df_s, df_r, rz_s, rz_r, rg_s, rg_r, c_s, c_r, x_s, x_r, z_s, z_r,
):
    n_pair, n_aux, n_occ, pairs, share, occ_rows, depth = sizes
    n_group = n_aux * n_occ
    me, a, c = lax.axis_index("pair"), lax.axis_index("aux"), lax.axis_index("occ")
    g = a * n_occ + c
    other = 1 - c

    def pair_peer(k):
        return lax.rem(me + k, n_pair)

    def group_peer(j):
        peer = lax.rem(g + j, n_group)
        return {"aux": peer // n_occ, "occ": lax.rem(peer, n_occ)}

    def aux_peer(j):
        return lax.rem(a + j, n_aux)

    def remote(src, dst, send, recv, device):
        return pltpu.make_async_remote_copy(
            src_ref=src, dst_ref=dst, send_sem=send, recv_sem=recv,
            device_id=device, device_id_type=MESH,
        )

    barrier = pltpu.get_barrier_semaphore()
    for k in range(1, n_pair):
        pl.semaphore_signal(barrier, inc=1, device_id={"pair": pair_peer(k)}, device_id_type=MESH)
    for j in range(1, n_group):
        pl.semaphore_signal(barrier, inc=1, device_id=group_peer(j), device_id_type=MESH)
    pl.semaphore_wait(barrier, n_pair + n_group - 2)

    own_df = pltpu.make_async_copy(
        df.at[:, pl.ds(me * depth, depth), :], dfb.at[pl.ds(me * occ_rows, occ_rows)], local_sem.at[0]
    )
    own_rot = pltpu.make_async_copy(rot.at[g], rotb.at[me, g], local_sem.at[1])
    own_rot.start()
    rot_z = [
        remote(rot.at[g], rotb.at[me, g], rz_s.at[k], rz_r.at[k], {"pair": pair_peer(k)})
        for k in range(1, n_pair)
    ]
    for copy in rot_z:
        copy.start()
    moves = []
    for k in range(1, n_pair):
        peer = pair_peer(k)
        moves.append(remote(
            df.at[:, pl.ds(peer * depth, depth), :], dfb.at[pl.ds(me * occ_rows, occ_rows)],
            df_s.at[k], df_r.at[k], {"pair": peer},
        ))
        moves[-1].start()
    own_df.start()
    own_rot.wait()
    for copy in rot_z:
        copy.wait()
    rot_g = [
        remote(rotb.at[:, g], rotb.at[:, g], rg_s.at[j], rg_r.at[j], group_peer(j))
        for j in range(1, n_group)
    ]
    for copy in rot_g:
        copy.start()
    for copy in rot_g:
        copy.wait()
    own_df.wait()
    for copy in moves:
        copy.wait()

    def owner_of(t):
        return lax.rem(me + 1 + t, n_pair)

    def core_copy(t):
        return remote(
            ex.at[t % 2, :, :, other], crecv.at[t], c_s.at[t], c_r.at[t], {"occ": other}
        )

    def aux_copy(t, j):
        return remote(
            xsend.at[t % 2, j - 1], xrecv.at[t, j - 1], x_s.at[t, j - 1], x_r.at[t, j - 1],
            {"aux": aux_peer(j)},
        )

    def owner_copy(t):
        return remote(zsend.at[t], zrecv.at[t], z_s.at[t], z_r.at[t], {"pair": owner_of(t)})

    def contract(t):
        owner = owner_of(t)

        def one(p, carry):
            row = (owner * pairs + p) * 2
            left, right = dfb[idx[row]], dfb[idx[row + 1]]
            turn = rotb[owner, p // share, lax.rem(p, share)]
            left = jnp.dot(left, turn, preferred_element_type=jnp.float32).astype(jnp.bfloat16)
            right = jnp.dot(right, turn, preferred_element_type=jnp.float32).astype(jnp.bfloat16)
            both = lax.dot_general(
                left, right, (((0,), (0,)), ((), ())), preferred_element_type=jnp.float32
            )
            ex[t % 2, p] = both.reshape(ex.shape[2:])
            return carry

        lax.fori_loop(0, pairs, one, 0)
        core_copy(t).start()

    def add_core(t):
        core_copy(t).wait()
        for j in range(1, n_aux):
            peer = aux_peer(j)
            xsend[t % 2, j - 1] = (ex[t % 2, :, peer, c] + crecv[t, :, peer]).astype(jnp.bfloat16)
            aux_copy(t, j).start()
        crecv[t, :, a] = crecv[t, :, a] + ex[t % 2, :, a, c]

    def add_aux(t):
        total = crecv[t, :, a]
        for j in range(1, n_aux):
            aux_copy(t, j).wait()
            total = total + xrecv[t, j - 1].astype(jnp.float32)
        if t < n_pair - 1:
            zsend[t] = total.astype(jnp.bfloat16)
            owner_copy(t).start()
        else:
            out[...] = total

    for t in range(n_pair + 2):
        if t < n_pair:
            contract(t)
        if 1 <= t < n_pair + 1:
            add_core(t - 1)
        if t >= 2:
            add_aux(t - 2)
    for t in range(n_pair - 1):
        owner_copy(t).wait()
        out[...] += zrecv[t].astype(jnp.float32)


def exchange_sum(df_ints, pno_rot, orbital, band_rows):
    n_pair, n_aux, n_occ = lax.axis_size("pair"), lax.axis_size("aux"), lax.axis_size("occ")
    n_group = n_aux * n_occ
    pairs, width = pno_rot.shape[0], pno_rot.shape[1]
    share = pairs // n_group
    occ_rows, fit_rows = df_ints.shape[0], df_ints.shape[1]
    depth = fit_rows // n_pair
    sizes = (n_pair, n_aux, n_occ, pairs, share, occ_rows, depth)
    bf16, f32, dma = jnp.bfloat16, jnp.float32, pltpu.SemaphoreType.DMA
    block = (pairs, band_rows, width)
    others = max(1, n_aux - 1)
    flops = 6 * n_pair * pairs * depth * width * width
    return pl.pallas_call(
        functools.partial(exchange_kernel, sizes),
        out_shape=jax.ShapeDtypeStruct(block, f32),
        in_specs=[
            pl.BlockSpec(memory_space=pl.ANY),
            pl.BlockSpec(memory_space=pl.ANY),
            pl.BlockSpec(memory_space=pltpu.SMEM),
        ],
        out_specs=pl.BlockSpec(memory_space=pltpu.VMEM),
        scratch_shapes=[
            pltpu.VMEM((n_pair * occ_rows, depth, width), bf16),
            pltpu.VMEM((n_pair, n_group, share, width, width), bf16),
            pltpu.VMEM((2, pairs, n_aux, n_occ, band_rows, width), f32),
            pltpu.VMEM((n_pair, pairs, n_aux, band_rows, width), f32),
            pltpu.VMEM((2, others) + block, bf16),
            pltpu.VMEM((n_pair, others) + block, bf16),
            pltpu.VMEM((n_pair,) + block, bf16),
            pltpu.VMEM((n_pair,) + block, bf16),
            dma((2,)),
            dma((n_pair,)), dma((n_pair,)),
            dma((n_pair,)), dma((n_pair,)),
            dma((n_group,)), dma((n_group,)),
            dma((n_pair,)), dma((n_pair,)),
            dma((n_pair, others)), dma((n_pair, others)),
            dma((n_pair,)), dma((n_pair,)),
        ],
        compiler_params=pltpu.CompilerParams(
            collective_id=0, has_side_effects=True, vmem_limit_bytes=58 << 20
        ),
        cost_estimate=pl.CostEstimate(
            flops=flops, bytes_accessed=400 << 20, transcendentals=0
        ),
    )(df_ints, pno_rot.reshape(n_group, share, width, width), orbital.reshape(-1))


def body(
    df_ints,
    pno_rot,
    margins,
    amplitudes,
    virt_energy,
    occ_gap,
    fock_coupling,
    pno_count,
    pair_home,
    pair_slot,
    neigh_home,
    neigh_slot,
):
    own_index = lax.axis_index("pair")
    group_index = lax.axis_index(("aux", "occ"))
    pairs_here, pno_width = pno_rot.shape[0], pno_rot.shape[1]
    occ_rows = df_ints.shape[0]
    band_rows = amplitudes.shape[1]
    neigh_count = margins.shape[1]
    orbital = pair_home * occ_rows + pair_slot
    own_homes = lax.dynamic_slice_in_dim(neigh_home, own_index * pairs_here, pairs_here, 0)
    own_slots = lax.dynamic_slice_in_dim(neigh_slot, own_index * pairs_here, pairs_here, 0)
    partner = own_homes * pairs_here + own_slots

    exchange_rows = exchange_sum(df_ints, pno_rot, orbital, band_rows)

    amp_all = lax.all_gather(amplitudes.astype(jnp.bfloat16), "pair", axis=0, tiled=True)
    picked = jnp.take(amp_all, partner, axis=0)
    neighbour = lax.all_gather(picked, ("aux", "occ"), axis=2, tiled=True)
    row_start = group_index * band_rows
    margin_rows = lax.dynamic_slice_in_dim(margins, row_start, band_rows, axis=2)
    projected = jnp.einsum(
        "pkrv,pkvb->pkrb", margin_rows, neighbour, preferred_element_type=jnp.float32
    ).astype(jnp.bfloat16)
    coupled = jnp.einsum("pkrb,pkcb->pkrc", projected, margins, preferred_element_type=jnp.float32)
    coupling = jnp.sum(fock_coupling[:, :, None, None] * coupled, axis=1)
    energy_rows = lax.dynamic_slice_in_dim(virt_energy, row_start, band_rows, axis=1)
    denominator = energy_rows[:, :, None] + virt_energy[:, None, :] + occ_gap[:, None, None]
    residual = exchange_rows + denominator * amplitudes - coupling
    row_pos = row_start + jnp.arange(band_rows, dtype=jnp.int32)
    col_pos = jnp.arange(pno_width, dtype=jnp.int32)
    counts = pno_count[:, None, None]
    active = (row_pos[None, :, None] < counts) & (col_pos[None, None, :] < counts)
    updated = jnp.where(
        active, amplitudes - 0.5 * residual / denominator, jnp.zeros_like(amplitudes)
    )
    energy_part = jnp.sum(exchange_rows * updated, axis=(1, 2))
    pair_energy = lax.psum(energy_part, ("aux", "occ")) / pno_width
    return (updated, pair_energy)


def solution(mesh):
    placed = (
        P(("grp", "pair"), ("aux", "occ"), None),
        P(("grp", "pair"), None, None),
        P(("grp", "pair"), None, None, None),
        P(("grp", "pair"), ("aux", "occ"), None),
        P(("grp", "pair"), None),
        P(("grp", "pair")),
        P(("grp", "pair"), None),
        P(("grp", "pair")),
        P("grp", None),
        P("grp", None),
        P("grp", None),
        P("grp", None),
    )
    return jax.shard_map(
        body,
        mesh=mesh,
        in_specs=placed,
        out_specs=(P(("grp", "pair"), ("aux", "occ"), None), P(("grp", "pair"))),
        check_vma=False,
    )
```

```python
import functools

import jax
import jax.numpy as jnp
from jax import lax
from jax.experimental import pallas as pl
from jax.experimental.pallas import tpu as pltpu
from jax.sharding import PartitionSpec as P


MESH = pl.DeviceIdType.MESH


def exchange_kernel(
    sizes, df, rot, idx, amp, out, amp_all,
    dfb, rotb, ex, crecv, xsend, xrecv, zsend, zrecv,
    local_sem, df_s, df_r, rz_s, rz_r, rg_s, rg_r, c_s, c_r, x_s, x_r, z_s, z_r,
    az_s, az_r, ag_s, ag_r,
):
    n_pair, n_aux, n_occ, pairs, share, occ_rows, depth = sizes
    n_group = n_aux * n_occ
    me, a, c = lax.axis_index("pair"), lax.axis_index("aux"), lax.axis_index("occ")
    g = a * n_occ + c
    other = 1 - c

    def pair_peer(k):
        return lax.rem(me + k, n_pair)

    def group_peer(j):
        peer = lax.rem(g + j, n_group)
        return {"aux": peer // n_occ, "occ": lax.rem(peer, n_occ)}

    def aux_peer(j):
        return lax.rem(a + j, n_aux)

    def remote(src, dst, send, recv, device):
        return pltpu.make_async_remote_copy(
            src_ref=src, dst_ref=dst, send_sem=send, recv_sem=recv,
            device_id=device, device_id_type=MESH,
        )

    barrier = pltpu.get_barrier_semaphore()
    for k in range(1, n_pair):
        pl.semaphore_signal(barrier, inc=1, device_id={"pair": pair_peer(k)}, device_id_type=MESH)
    for j in range(1, n_group):
        pl.semaphore_signal(barrier, inc=1, device_id=group_peer(j), device_id_type=MESH)
    pl.semaphore_wait(barrier, n_pair + n_group - 2)

    own_df = pltpu.make_async_copy(
        df.at[:, pl.ds(me * depth, depth), :], dfb.at[pl.ds(me * occ_rows, occ_rows)], local_sem.at[0]
    )
    own_rot = pltpu.make_async_copy(rot.at[g], rotb.at[me, g], local_sem.at[1])
    own_rot.start()
    rot_z = [
        remote(rot.at[g], rotb.at[me, g], rz_s.at[k], rz_r.at[k], {"pair": pair_peer(k)})
        for k in range(1, n_pair)
    ]
    for copy in rot_z:
        copy.start()
    moves = []
    for k in range(1, n_pair):
        peer = pair_peer(k)
        moves.append(remote(
            df.at[:, pl.ds(peer * depth, depth), :], dfb.at[pl.ds(me * occ_rows, occ_rows)],
            df_s.at[k], df_r.at[k], {"pair": peer},
        ))
        moves[-1].start()
    own_df.start()
    own_rot.wait()
    for copy in rot_z:
        copy.wait()
    rot_g = [
        remote(rotb.at[:, g], rotb.at[:, g], rg_s.at[j], rg_r.at[j], group_peer(j))
        for j in range(1, n_group)
    ]
    for copy in rot_g:
        copy.start()
    for copy in rot_g:
        copy.wait()
    own_df.wait()
    for copy in moves:
        copy.wait()

    def owner_of(t):
        return lax.rem(me + 1 + t, n_pair)

    def core_copy(t):
        return remote(
            ex.at[t % 2, :, :, other], crecv.at[t], c_s.at[t], c_r.at[t], {"occ": other}
        )

    def aux_copy(t, j):
        return remote(
            xsend.at[t % 2, j - 1], xrecv.at[t, j - 1], x_s.at[t, j - 1], x_r.at[t, j - 1],
            {"aux": aux_peer(j)},
        )

    def owner_copy(t):
        return remote(zsend.at[t], zrecv.at[t], z_s.at[t], z_r.at[t], {"pair": owner_of(t)})

    def contract(t):
        owner = owner_of(t)

        def one(p, carry):
            row = (owner * pairs + p) * 2
            left, right = dfb[idx[row]], dfb[idx[row + 1]]
            turn = rotb[owner, p // share, lax.rem(p, share)]
            left = jnp.dot(left, turn, preferred_element_type=jnp.float32).astype(jnp.bfloat16)
            right = jnp.dot(right, turn, preferred_element_type=jnp.float32).astype(jnp.bfloat16)
            both = lax.dot_general(
                left, right, (((0,), (0,)), ((), ())), preferred_element_type=jnp.float32
            )
            ex[t % 2, p] = both.reshape(ex.shape[2:])
            return carry

        lax.fori_loop(0, pairs, one, 0)
        core_copy(t).start()

    def add_core(t):
        core_copy(t).wait()
        for j in range(1, n_aux):
            peer = aux_peer(j)
            xsend[t % 2, j - 1] = (ex[t % 2, :, peer, c] + crecv[t, :, peer]).astype(jnp.bfloat16)
            aux_copy(t, j).start()
        crecv[t, :, a] = crecv[t, :, a] + ex[t % 2, :, a, c]

    def add_aux(t):
        total = crecv[t, :, a]
        for j in range(1, n_aux):
            aux_copy(t, j).wait()
            total = total + xrecv[t, j - 1].astype(jnp.float32)
        if t < n_pair - 1:
            zsend[t] = total.astype(jnp.bfloat16)
            owner_copy(t).start()
        else:
            out[...] = total

    own_amp = pltpu.make_async_copy(amp, amp_all.at[me, g], local_sem.at[2])
    own_amp.start()
    amp_z = [
        remote(amp, amp_all.at[me, g], az_s.at[k], az_r.at[k], {"pair": pair_peer(k)})
        for k in range(1, n_pair)
    ]
    amp_g = [
        remote(amp_all.at[:, g], amp_all.at[:, g], ag_s.at[j], ag_r.at[j], group_peer(j))
        for j in range(1, n_group)
    ]
    for copy in amp_z:
        copy.start()

    for t in range(n_pair + 2):
        if t == n_pair - 1:
            own_amp.wait()
            for copy in amp_z:
                copy.wait()
            for copy in amp_g:
                copy.start()
        if t < n_pair:
            contract(t)
        if 1 <= t < n_pair + 1:
            add_core(t - 1)
        if t >= 2:
            add_aux(t - 2)
    for t in range(n_pair - 1):
        owner_copy(t).wait()
        out[...] += zrecv[t].astype(jnp.float32)
    for copy in amp_g:
        copy.wait()


def exchange_sum(df_ints, pno_rot, orbital, amp_wire):
    n_pair, n_aux, n_occ = lax.axis_size("pair"), lax.axis_size("aux"), lax.axis_size("occ")
    n_group = n_aux * n_occ
    pairs, width = pno_rot.shape[0], pno_rot.shape[1]
    share = pairs // n_group
    occ_rows, fit_rows = df_ints.shape[0], df_ints.shape[1]
    depth = fit_rows // n_pair
    sizes = (n_pair, n_aux, n_occ, pairs, share, occ_rows, depth)
    bf16, f32, dma = jnp.bfloat16, jnp.float32, pltpu.SemaphoreType.DMA
    block = amp_wire.shape
    band_rows = block[1]
    others = max(1, n_aux - 1)
    flops = 6 * n_pair * pairs * depth * width * width
    return pl.pallas_call(
        functools.partial(exchange_kernel, sizes),
        out_shape=(
            jax.ShapeDtypeStruct(block, f32),
            jax.ShapeDtypeStruct((n_pair, n_group) + block, bf16),
        ),
        in_specs=[
            pl.BlockSpec(memory_space=pl.ANY),
            pl.BlockSpec(memory_space=pl.ANY),
            pl.BlockSpec(memory_space=pltpu.SMEM),
            pl.BlockSpec(memory_space=pl.ANY),
        ],
        out_specs=(
            pl.BlockSpec(memory_space=pltpu.VMEM),
            pl.BlockSpec(memory_space=pl.ANY),
        ),
        scratch_shapes=[
            pltpu.VMEM((n_pair * occ_rows, depth, width), bf16),
            pltpu.VMEM((n_pair, n_group, share, width, width), bf16),
            pltpu.VMEM((2, pairs, n_aux, n_occ, band_rows, width), f32),
            pltpu.VMEM((n_pair, pairs, n_aux, band_rows, width), f32),
            pltpu.VMEM((2, others) + block, bf16),
            pltpu.VMEM((n_pair, others) + block, bf16),
            pltpu.VMEM((n_pair,) + block, bf16),
            pltpu.VMEM((n_pair,) + block, bf16),
            dma((3,)),
            dma((n_pair,)), dma((n_pair,)),
            dma((n_pair,)), dma((n_pair,)),
            dma((n_group,)), dma((n_group,)),
            dma((n_pair,)), dma((n_pair,)),
            dma((n_pair, others)), dma((n_pair, others)),
            dma((n_pair,)), dma((n_pair,)),
            dma((n_pair,)), dma((n_pair,)),
            dma((n_group,)), dma((n_group,)),
        ],
        compiler_params=pltpu.CompilerParams(
            collective_id=0, has_side_effects=True, vmem_limit_bytes=58 << 20
        ),
        cost_estimate=pl.CostEstimate(
            flops=flops, bytes_accessed=400 << 20, transcendentals=0
        ),
    )(df_ints, pno_rot.reshape(n_group, share, width, width), orbital.reshape(-1), amp_wire)


def body(
    df_ints,
    pno_rot,
    margins,
    amplitudes,
    virt_energy,
    occ_gap,
    fock_coupling,
    pno_count,
    pair_home,
    pair_slot,
    neigh_home,
    neigh_slot,
):
    own_index = lax.axis_index("pair")
    group_index = lax.axis_index(("aux", "occ"))
    pairs_here, pno_width = pno_rot.shape[0], pno_rot.shape[1]
    occ_rows = df_ints.shape[0]
    band_rows = amplitudes.shape[1]
    neigh_count = margins.shape[1]
    orbital = pair_home * occ_rows + pair_slot
    own_homes = lax.dynamic_slice_in_dim(neigh_home, own_index * pairs_here, pairs_here, 0)
    own_slots = lax.dynamic_slice_in_dim(neigh_slot, own_index * pairs_here, pairs_here, 0)

    exchange_rows, amp_all = exchange_sum(
        df_ints, pno_rot, orbital, amplitudes.astype(jnp.bfloat16)
    )
    neighbour = amp_all[own_homes, :, own_slots].reshape(
        pairs_here, neigh_count, pno_width, pno_width
    )
    row_start = group_index * band_rows
    margin_rows = lax.dynamic_slice_in_dim(margins, row_start, band_rows, axis=2)
    projected = jnp.einsum(
        "pkrv,pkvb->pkrb", margin_rows, neighbour, preferred_element_type=jnp.float32
    ).astype(jnp.bfloat16)
    coupled = jnp.einsum("pkrb,pkcb->pkrc", projected, margins, preferred_element_type=jnp.float32)
    coupling = jnp.sum(fock_coupling[:, :, None, None] * coupled, axis=1)
    energy_rows = lax.dynamic_slice_in_dim(virt_energy, row_start, band_rows, axis=1)
    denominator = energy_rows[:, :, None] + virt_energy[:, None, :] + occ_gap[:, None, None]
    residual = exchange_rows + denominator * amplitudes - coupling
    row_pos = row_start + jnp.arange(band_rows, dtype=jnp.int32)
    col_pos = jnp.arange(pno_width, dtype=jnp.int32)
    counts = pno_count[:, None, None]
    active = (row_pos[None, :, None] < counts) & (col_pos[None, None, :] < counts)
    updated = jnp.where(
        active, amplitudes - 0.5 * residual / denominator, jnp.zeros_like(amplitudes)
    )
    energy_part = jnp.sum(exchange_rows * updated, axis=(1, 2))
    pair_energy = lax.psum(energy_part, ("aux", "occ")) / pno_width
    return (updated, pair_energy)


def solution(mesh):
    placed = (
        P(("grp", "pair"), ("aux", "occ"), None),
        P(("grp", "pair"), None, None),
        P(("grp", "pair"), None, None, None),
        P(("grp", "pair"), ("aux", "occ"), None),
        P(("grp", "pair"), None),
        P(("grp", "pair")),
        P(("grp", "pair"), None),
        P(("grp", "pair")),
        P("grp", None),
        P("grp", None),
        P("grp", None),
        P("grp", None),
    )
    return jax.shard_map(
        body,
        mesh=mesh,
        in_specs=placed,
        out_specs=(P(("grp", "pair"), ("aux", "occ"), None), P(("grp", "pair"))),
        check_vma=False,
    )
```

```python
import functools

import jax
import jax.numpy as jnp
from jax import lax
from jax.experimental import pallas as pl
from jax.experimental.pallas import tpu as pltpu
from jax.sharding import PartitionSpec as P


MESH = pl.DeviceIdType.MESH


def exchange_kernel(
    sizes, df, rot, idx, amp, out, amp_all,
    dfb, rotb, ex, crecv, xsend, xrecv, zsend, zrecv,
    local_sem, df_s, df_r, rz_s, rz_r, rg_s, rg_r, c_s, c_r, x_s, x_r, z_s, z_r,
    az_s, az_r, ag_s, ag_r,
):
    n_pair, n_aux, n_occ, pairs, share, occ_rows, depth = sizes
    n_group = n_aux * n_occ
    me, a, c = lax.axis_index("pair"), lax.axis_index("aux"), lax.axis_index("occ")
    g = a * n_occ + c
    other = 1 - c

    def pair_peer(k):
        return lax.rem(me + k, n_pair)

    def group_peer(j):
        peer = lax.rem(g + j, n_group)
        return {"aux": peer // n_occ, "occ": lax.rem(peer, n_occ)}

    def aux_peer(j):
        return lax.rem(a + j, n_aux)

    def remote(src, dst, send, recv, device):
        return pltpu.make_async_remote_copy(
            src_ref=src, dst_ref=dst, send_sem=send, recv_sem=recv,
            device_id=device, device_id_type=MESH,
        )

    barrier = pltpu.get_barrier_semaphore()
    for k in range(1, n_pair):
        pl.semaphore_signal(barrier, inc=1, device_id={"pair": pair_peer(k)}, device_id_type=MESH)
    for j in range(1, n_group):
        pl.semaphore_signal(barrier, inc=1, device_id=group_peer(j), device_id_type=MESH)
    pl.semaphore_wait(barrier, n_pair + n_group - 2)

    own_df = pltpu.make_async_copy(
        df.at[:, pl.ds(me * depth, depth), :], dfb.at[pl.ds(me * occ_rows, occ_rows)], local_sem.at[0]
    )
    own_rot = pltpu.make_async_copy(rot.at[g], rotb.at[me, g], local_sem.at[1])
    own_amp = pltpu.make_async_copy(amp, amp_all.at[me, g], local_sem.at[2])
    own_rot.start()
    own_amp.start()
    own_rot.wait()
    own_amp.wait()

    def doubling(far):
        near = far * 2
        peer = me + far * (1 - 2 * lax.rem(me // far, 2))
        copies = []
        for i in range(n_pair // near):
            block, sem = lax.rem(me, near) + near * i, n_pair // near + i
            for table, send, recv in ((rotb, rz_s, rz_r), (amp_all, az_s, az_r)):
                ref = table.at[block, g]
                copies.append(remote(ref, ref, send.at[sem], recv.at[sem], {"pair": peer}))
        return copies

    hops = [n_pair >> (b + 1) for b in range(n_pair.bit_length() - 1)]
    flying = doubling(hops[0])
    for copy in flying:
        copy.start()
    moves = []
    for k in range(1, n_pair):
        peer = pair_peer(k)
        moves.append(remote(
            df.at[:, pl.ds(peer * depth, depth), :], dfb.at[pl.ds(me * occ_rows, occ_rows)],
            df_s.at[k], df_r.at[k], {"pair": peer},
        ))
        moves[-1].start()
    own_df.start()
    for hop in hops[1:]:
        for copy in flying:
            copy.wait()
        flying = doubling(hop)
        for copy in flying:
            copy.start()
    for copy in flying:
        copy.wait()
    rot_g = [
        remote(rotb.at[:, g], rotb.at[:, g], rg_s.at[j], rg_r.at[j], group_peer(j))
        for j in range(1, n_group)
    ]
    amp_g = [
        remote(amp_all.at[:, g], amp_all.at[:, g], ag_s.at[j], ag_r.at[j], group_peer(j))
        for j in range(1, n_group)
    ]
    for copy in rot_g + amp_g:
        copy.start()
    for copy in rot_g + amp_g:
        copy.wait()
    own_df.wait()
    for copy in moves:
        copy.wait()

    def owner_of(t):
        return lax.rem(me + 1 + t, n_pair)

    def core_copy(t):
        return remote(
            ex.at[t % 2, :, :, other], crecv.at[t], c_s.at[t], c_r.at[t], {"occ": other}
        )

    def aux_copy(t, j):
        return remote(
            xsend.at[t % 2, j - 1], xrecv.at[t, j - 1], x_s.at[t, j - 1], x_r.at[t, j - 1],
            {"aux": aux_peer(j)},
        )

    def owner_copy(t):
        return remote(zsend.at[t], zrecv.at[t], z_s.at[t], z_r.at[t], {"pair": owner_of(t)})

    def contract(t):
        owner = owner_of(t)

        def one(p, carry):
            row = (owner * pairs + p) * 2
            left, right = dfb[idx[row]], dfb[idx[row + 1]]
            turn = rotb[owner, p // share, lax.rem(p, share)]
            left = jnp.dot(left, turn, preferred_element_type=jnp.float32).astype(jnp.bfloat16)
            right = jnp.dot(right, turn, preferred_element_type=jnp.float32).astype(jnp.bfloat16)
            both = lax.dot_general(
                left, right, (((0,), (0,)), ((), ())), preferred_element_type=jnp.float32
            )
            ex[t % 2, p] = both.reshape(ex.shape[2:])
            return carry

        lax.fori_loop(0, pairs, one, 0)
        core_copy(t).start()

    def add_core(t):
        core_copy(t).wait()
        for j in range(1, n_aux):
            peer = aux_peer(j)
            xsend[t % 2, j - 1] = (ex[t % 2, :, peer, c] + crecv[t, :, peer]).astype(jnp.bfloat16)
            aux_copy(t, j).start()
        crecv[t, :, a] = crecv[t, :, a] + ex[t % 2, :, a, c]

    def add_aux(t):
        total = crecv[t, :, a]
        for j in range(1, n_aux):
            aux_copy(t, j).wait()
            total = total + xrecv[t, j - 1].astype(jnp.float32)
        if t < n_pair - 1:
            zsend[t] = total.astype(jnp.bfloat16)
            owner_copy(t).start()
        else:
            out[...] = total

    for t in range(n_pair + 2):
        if t < n_pair:
            contract(t)
        if 1 <= t < n_pair + 1:
            add_core(t - 1)
        if t >= 2:
            add_aux(t - 2)
    for t in range(n_pair - 1):
        owner_copy(t).wait()
        out[...] += zrecv[t].astype(jnp.float32)


def exchange_sum(df_ints, pno_rot, orbital, amp_wire):
    n_pair, n_aux, n_occ = lax.axis_size("pair"), lax.axis_size("aux"), lax.axis_size("occ")
    n_group = n_aux * n_occ
    pairs, width = pno_rot.shape[0], pno_rot.shape[1]
    share = pairs // n_group
    occ_rows, fit_rows = df_ints.shape[0], df_ints.shape[1]
    depth = fit_rows // n_pair
    sizes = (n_pair, n_aux, n_occ, pairs, share, occ_rows, depth)
    bf16, f32, dma = jnp.bfloat16, jnp.float32, pltpu.SemaphoreType.DMA
    block = amp_wire.shape
    band_rows = block[1]
    others = max(1, n_aux - 1)
    flops = 6 * n_pair * pairs * depth * width * width
    return pl.pallas_call(
        functools.partial(exchange_kernel, sizes),
        out_shape=(
            jax.ShapeDtypeStruct(block, f32),
            jax.ShapeDtypeStruct((n_pair, n_group) + block, bf16),
        ),
        in_specs=[
            pl.BlockSpec(memory_space=pl.ANY),
            pl.BlockSpec(memory_space=pl.ANY),
            pl.BlockSpec(memory_space=pltpu.SMEM),
            pl.BlockSpec(memory_space=pl.ANY),
        ],
        out_specs=(
            pl.BlockSpec(memory_space=pltpu.VMEM),
            pl.BlockSpec(memory_space=pl.ANY),
        ),
        scratch_shapes=[
            pltpu.VMEM((n_pair * occ_rows, depth, width), bf16),
            pltpu.VMEM((n_pair, n_group, share, width, width), bf16),
            pltpu.VMEM((2, pairs, n_aux, n_occ, band_rows, width), f32),
            pltpu.VMEM((n_pair, pairs, n_aux, band_rows, width), f32),
            pltpu.VMEM((2, others) + block, bf16),
            pltpu.VMEM((n_pair, others) + block, bf16),
            pltpu.VMEM((n_pair,) + block, bf16),
            pltpu.VMEM((n_pair,) + block, bf16),
            dma((3,)),
            dma((n_pair,)), dma((n_pair,)),
            dma((n_pair,)), dma((n_pair,)),
            dma((n_group,)), dma((n_group,)),
            dma((n_pair,)), dma((n_pair,)),
            dma((n_pair, others)), dma((n_pair, others)),
            dma((n_pair,)), dma((n_pair,)),
            dma((n_pair,)), dma((n_pair,)),
            dma((n_group,)), dma((n_group,)),
        ],
        compiler_params=pltpu.CompilerParams(
            collective_id=0, has_side_effects=True, vmem_limit_bytes=58 << 20
        ),
        cost_estimate=pl.CostEstimate(
            flops=flops, bytes_accessed=400 << 20, transcendentals=0
        ),
    )(df_ints, pno_rot.reshape(n_group, share, width, width), orbital.reshape(-1), amp_wire)


def body(
    df_ints,
    pno_rot,
    margins,
    amplitudes,
    virt_energy,
    occ_gap,
    fock_coupling,
    pno_count,
    pair_home,
    pair_slot,
    neigh_home,
    neigh_slot,
):
    own_index = lax.axis_index("pair")
    group_index = lax.axis_index(("aux", "occ"))
    pairs_here, pno_width = pno_rot.shape[0], pno_rot.shape[1]
    occ_rows = df_ints.shape[0]
    band_rows = amplitudes.shape[1]
    neigh_count = margins.shape[1]
    orbital = pair_home * occ_rows + pair_slot
    own_homes = lax.dynamic_slice_in_dim(neigh_home, own_index * pairs_here, pairs_here, 0)
    own_slots = lax.dynamic_slice_in_dim(neigh_slot, own_index * pairs_here, pairs_here, 0)

    exchange_rows, amp_all = exchange_sum(
        df_ints, pno_rot, orbital, amplitudes.astype(jnp.bfloat16)
    )
    neighbour = amp_all[own_homes, :, own_slots].reshape(
        pairs_here, neigh_count, pno_width, pno_width
    )
    row_start = group_index * band_rows
    margin_rows = lax.dynamic_slice_in_dim(margins, row_start, band_rows, axis=2)
    projected = jnp.einsum(
        "pkrv,pkvb->pkrb", margin_rows, neighbour, preferred_element_type=jnp.float32
    ).astype(jnp.bfloat16)
    coupled = jnp.einsum("pkrb,pkcb->pkrc", projected, margins, preferred_element_type=jnp.float32)
    coupling = jnp.sum(fock_coupling[:, :, None, None] * coupled, axis=1)
    energy_rows = lax.dynamic_slice_in_dim(virt_energy, row_start, band_rows, axis=1)
    denominator = energy_rows[:, :, None] + virt_energy[:, None, :] + occ_gap[:, None, None]
    residual = exchange_rows + denominator * amplitudes - coupling
    row_pos = row_start + jnp.arange(band_rows, dtype=jnp.int32)
    col_pos = jnp.arange(pno_width, dtype=jnp.int32)
    counts = pno_count[:, None, None]
    active = (row_pos[None, :, None] < counts) & (col_pos[None, None, :] < counts)
    updated = jnp.where(
        active, amplitudes - 0.5 * residual / denominator, jnp.zeros_like(amplitudes)
    )
    energy_part = jnp.sum(exchange_rows * updated, axis=(1, 2))
    pair_energy = lax.psum(energy_part, ("aux", "occ")) / pno_width
    return (updated, pair_energy)


def solution(mesh):
    placed = (
        P(("grp", "pair"), ("aux", "occ"), None),
        P(("grp", "pair"), None, None),
        P(("grp", "pair"), None, None, None),
        P(("grp", "pair"), ("aux", "occ"), None),
        P(("grp", "pair"), None),
        P(("grp", "pair")),
        P(("grp", "pair"), None),
        P(("grp", "pair")),
        P("grp", None),
        P("grp", None),
        P("grp", None),
        P("grp", None),
    )
    return jax.shard_map(
        body,
        mesh=mesh,
        in_specs=placed,
        out_specs=(P(("grp", "pair"), ("aux", "occ"), None), P(("grp", "pair"))),
        check_vma=False,
    )
```

```python
import functools

import jax
import jax.numpy as jnp
from jax import lax
from jax.experimental import pallas as pl
from jax.experimental.pallas import tpu as pltpu
from jax.sharding import PartitionSpec as P


MESH = pl.DeviceIdType.MESH


def exchange_kernel(
    sizes, df, rot, idx, amp, out, amp_all,
    dfb, rotb, ex, crecv, xsend, xrecv, zsend, zrecv,
    local_sem, df_s, df_r, rz_s, rz_r, rg_s, rg_r, c_s, c_r, x_s, x_r, z_s, z_r,
    az_s, az_r, ag_s, ag_r,
):
    n_pair, n_aux, n_occ, pairs, share, occ_rows, depth = sizes
    n_group = n_aux * n_occ
    me, a, c = lax.axis_index("pair"), lax.axis_index("aux"), lax.axis_index("occ")
    g = a * n_occ + c
    other = 1 - c

    def pair_peer(k):
        return lax.rem(me + k, n_pair)

    def group_peer(j):
        peer = lax.rem(g + j, n_group)
        return {"aux": peer // n_occ, "occ": lax.rem(peer, n_occ)}

    def aux_peer(j):
        return lax.rem(a + j, n_aux)

    def remote(src, dst, send, recv, device):
        return pltpu.make_async_remote_copy(
            src_ref=src, dst_ref=dst, send_sem=send, recv_sem=recv,
            device_id=device, device_id_type=MESH,
        )

    barrier = pltpu.get_barrier_semaphore()
    for k in range(1, n_pair):
        pl.semaphore_signal(barrier, inc=1, device_id={"pair": pair_peer(k)}, device_id_type=MESH)
    for j in range(1, n_group):
        pl.semaphore_signal(barrier, inc=1, device_id=group_peer(j), device_id_type=MESH)
    pl.semaphore_wait(barrier, n_pair + n_group - 2)

    own_df = pltpu.make_async_copy(
        df.at[:, pl.ds(me * depth, depth), :], dfb.at[pl.ds(me * occ_rows, occ_rows)], local_sem.at[0]
    )
    own_rot = pltpu.make_async_copy(rot.at[g], rotb.at[me, g], local_sem.at[1])
    own_amp = pltpu.make_async_copy(amp, amp_all.at[me, g], local_sem.at[2])
    own_rot.start()
    own_amp.start()
    own_rot.wait()
    own_amp.wait()

    def doubling(far):
        near = far * 2
        peer = me + far * (1 - 2 * lax.rem(me // far, 2))
        copies = []
        for i in range(n_pair // near):
            block, sem = lax.rem(me, near) + near * i, n_pair // near + i
            for table, send, recv in ((rotb, rz_s, rz_r), (amp_all, az_s, az_r)):
                ref = table.at[block, g]
                copies.append(remote(ref, ref, send.at[sem], recv.at[sem], {"pair": peer}))
        return copies

    hops = [n_pair >> (b + 1) for b in range(n_pair.bit_length() - 1)]
    flying = doubling(hops[0])
    for copy in flying:
        copy.start()
    moves = []

    def send_df(first, count, part):
        for k in range(1, n_pair):
            peer = pair_peer(k)
            moves.append(remote(
                df.at[pl.ds(first, count), pl.ds(peer * depth, depth), :],
                dfb.at[pl.ds(me * occ_rows + first, count)],
                df_s.at[k, part], df_r.at[k, part], {"pair": peer},
            ))
            moves[-1].start()

    for part, hop in enumerate(hops[1:], 1):
        for copy in flying:
            copy.wait()
        flying = doubling(hop)
        for copy in flying:
            copy.start()
    for copy in flying:
        copy.wait()
    rot_g = [
        remote(rotb.at[:, g], rotb.at[:, g], rg_s.at[j], rg_r.at[j], group_peer(j))
        for j in range(1, n_group)
    ]
    amp_g = [
        remote(amp_all.at[:, g], amp_all.at[:, g], ag_s.at[j], ag_r.at[j], group_peer(j))
        for j in range(1, n_group)
    ]
    for copy in rot_g + amp_g:
        copy.start()
    send_df(0, occ_rows, 0)
    own_df.start()
    for copy in rot_g + amp_g:
        copy.wait()
    own_df.wait()
    for copy in moves:
        copy.wait()

    def owner_of(t):
        return lax.rem(me + 1 + t, n_pair)

    def core_copy(t):
        return remote(
            ex.at[t % 2, :, :, other], crecv.at[t], c_s.at[t], c_r.at[t], {"occ": other}
        )

    def aux_copy(t, j):
        return remote(
            xsend.at[t % 2, j - 1], xrecv.at[t, j - 1], x_s.at[t, j - 1], x_r.at[t, j - 1],
            {"aux": aux_peer(j)},
        )

    def owner_copy(t):
        return remote(zsend.at[t], zrecv.at[t], z_s.at[t], z_r.at[t], {"pair": owner_of(t)})

    def contract(t):
        owner = owner_of(t)

        def one(p, carry):
            row = (owner * pairs + p) * 2
            left, right = dfb[idx[row]], dfb[idx[row + 1]]
            turn = rotb[owner, p // share, lax.rem(p, share)]
            left = jnp.dot(left, turn, preferred_element_type=jnp.float32).astype(jnp.bfloat16)
            right = jnp.dot(right, turn, preferred_element_type=jnp.float32).astype(jnp.bfloat16)
            both = lax.dot_general(
                left, right, (((0,), (0,)), ((), ())), preferred_element_type=jnp.float32
            )
            ex[t % 2, p] = both.reshape(ex.shape[2:])
            return carry

        lax.fori_loop(0, pairs, one, 0)
        core_copy(t).start()

    def add_core(t):
        core_copy(t).wait()
        for j in range(1, n_aux):
            peer = aux_peer(j)
            xsend[t % 2, j - 1] = (ex[t % 2, :, peer, c] + crecv[t, :, peer]).astype(jnp.bfloat16)
            aux_copy(t, j).start()
        crecv[t, :, a] = crecv[t, :, a] + ex[t % 2, :, a, c]

    def add_aux(t):
        total = crecv[t, :, a]
        for j in range(1, n_aux):
            aux_copy(t, j).wait()
            total = total + xrecv[t, j - 1].astype(jnp.float32)
        if t < n_pair - 1:
            zsend[t] = total.astype(jnp.bfloat16)
            owner_copy(t).start()
        else:
            out[...] = total

    for t in range(n_pair + 2):
        if t < n_pair:
            contract(t)
        if 1 <= t < n_pair + 1:
            add_core(t - 1)
        if t >= 2:
            add_aux(t - 2)
    for t in range(n_pair - 1):
        owner_copy(t).wait()
        out[...] += zrecv[t].astype(jnp.float32)


def exchange_sum(df_ints, pno_rot, orbital, amp_wire):
    n_pair, n_aux, n_occ = lax.axis_size("pair"), lax.axis_size("aux"), lax.axis_size("occ")
    n_group = n_aux * n_occ
    pairs, width = pno_rot.shape[0], pno_rot.shape[1]
    share = pairs // n_group
    occ_rows, fit_rows = df_ints.shape[0], df_ints.shape[1]
    depth = fit_rows // n_pair
    sizes = (n_pair, n_aux, n_occ, pairs, share, occ_rows, depth)
    bf16, f32, dma = jnp.bfloat16, jnp.float32, pltpu.SemaphoreType.DMA
    block = amp_wire.shape
    band_rows = block[1]
    others = max(1, n_aux - 1)
    flops = 6 * n_pair * pairs * depth * width * width
    return pl.pallas_call(
        functools.partial(exchange_kernel, sizes),
        out_shape=(
            jax.ShapeDtypeStruct(block, f32),
            jax.ShapeDtypeStruct((n_pair, n_group) + block, bf16),
        ),
        in_specs=[
            pl.BlockSpec(memory_space=pl.ANY),
            pl.BlockSpec(memory_space=pl.ANY),
            pl.BlockSpec(memory_space=pltpu.SMEM),
            pl.BlockSpec(memory_space=pl.ANY),
        ],
        out_specs=(
            pl.BlockSpec(memory_space=pltpu.VMEM),
            pl.BlockSpec(memory_space=pl.ANY),
        ),
        scratch_shapes=[
            pltpu.VMEM((n_pair * occ_rows, depth, width), bf16),
            pltpu.VMEM((n_pair, n_group, share, width, width), bf16),
            pltpu.VMEM((2, pairs, n_aux, n_occ, band_rows, width), f32),
            pltpu.VMEM((n_pair, pairs, n_aux, band_rows, width), f32),
            pltpu.VMEM((2, others) + block, bf16),
            pltpu.VMEM((n_pair, others) + block, bf16),
            pltpu.VMEM((n_pair,) + block, bf16),
            pltpu.VMEM((n_pair,) + block, bf16),
            dma((3,)),
            dma((n_pair, n_pair.bit_length())), dma((n_pair, n_pair.bit_length())),
            dma((n_pair,)), dma((n_pair,)),
            dma((n_group,)), dma((n_group,)),
            dma((n_pair,)), dma((n_pair,)),
            dma((n_pair, others)), dma((n_pair, others)),
            dma((n_pair,)), dma((n_pair,)),
            dma((n_pair,)), dma((n_pair,)),
            dma((n_group,)), dma((n_group,)),
        ],
        compiler_params=pltpu.CompilerParams(
            collective_id=0, has_side_effects=True, vmem_limit_bytes=58 << 20
        ),
        cost_estimate=pl.CostEstimate(
            flops=flops, bytes_accessed=400 << 20, transcendentals=0
        ),
    )(df_ints, pno_rot.reshape(n_group, share, width, width), orbital.reshape(-1), amp_wire)


def body(
    df_ints,
    pno_rot,
    margins,
    amplitudes,
    virt_energy,
    occ_gap,
    fock_coupling,
    pno_count,
    pair_home,
    pair_slot,
    neigh_home,
    neigh_slot,
):
    own_index = lax.axis_index("pair")
    group_index = lax.axis_index(("aux", "occ"))
    pairs_here, pno_width = pno_rot.shape[0], pno_rot.shape[1]
    occ_rows = df_ints.shape[0]
    band_rows = amplitudes.shape[1]
    neigh_count = margins.shape[1]
    orbital = pair_home * occ_rows + pair_slot
    own_homes = lax.dynamic_slice_in_dim(neigh_home, own_index * pairs_here, pairs_here, 0)
    own_slots = lax.dynamic_slice_in_dim(neigh_slot, own_index * pairs_here, pairs_here, 0)

    exchange_rows, amp_all = exchange_sum(
        df_ints, pno_rot, orbital, amplitudes.astype(jnp.bfloat16)
    )
    neighbour = amp_all[own_homes, :, own_slots].reshape(
        pairs_here, neigh_count, pno_width, pno_width
    )
    row_start = group_index * band_rows
    margin_rows = lax.dynamic_slice_in_dim(margins, row_start, band_rows, axis=2)
    projected = jnp.einsum(
        "pkrv,pkvb->pkrb", margin_rows, neighbour, preferred_element_type=jnp.float32
    ).astype(jnp.bfloat16)
    coupled = jnp.einsum("pkrb,pkcb->pkrc", projected, margins, preferred_element_type=jnp.float32)
    coupling = jnp.sum(fock_coupling[:, :, None, None] * coupled, axis=1)
    energy_rows = lax.dynamic_slice_in_dim(virt_energy, row_start, band_rows, axis=1)
    denominator = energy_rows[:, :, None] + virt_energy[:, None, :] + occ_gap[:, None, None]
    residual = exchange_rows + denominator * amplitudes - coupling
    row_pos = row_start + jnp.arange(band_rows, dtype=jnp.int32)
    col_pos = jnp.arange(pno_width, dtype=jnp.int32)
    counts = pno_count[:, None, None]
    active = (row_pos[None, :, None] < counts) & (col_pos[None, None, :] < counts)
    updated = jnp.where(
        active, amplitudes - 0.5 * residual / denominator, jnp.zeros_like(amplitudes)
    )
    energy_part = jnp.sum(exchange_rows * updated, axis=(1, 2))
    pair_energy = lax.psum(energy_part, ("aux", "occ")) / pno_width
    return (updated, pair_energy)


def solution(mesh):
    placed = (
        P(("grp", "pair"), ("aux", "occ"), None),
        P(("grp", "pair"), None, None),
        P(("grp", "pair"), None, None, None),
        P(("grp", "pair"), ("aux", "occ"), None),
        P(("grp", "pair"), None),
        P(("grp", "pair")),
        P(("grp", "pair"), None),
        P(("grp", "pair")),
        P("grp", None),
        P("grp", None),
        P("grp", None),
        P("grp", None),
    )
    return jax.shard_map(
        body,
        mesh=mesh,
        in_specs=placed,
        out_specs=(P(("grp", "pair"), ("aux", "occ"), None), P(("grp", "pair"))),
        check_vma=False,
    )
```
